32 devices in a mesh: seq: 8 (over z, core), mp: 4 (over y, x).
Axes of the slice: x: 2, y: 2, z: 4, core: 2. Of those that a mesh axis runs over, the one named last changes fastest.
Arguments:
- tokens: bfloat16 [128, 8192], P('seq', 'mp'), may hold values from -6 to 6
- gate_code: bfloat16 [8192, 16384], P('mp', 'seq'), may hold values from -4 to 4
- gate_scale: float32 [64, 128], P('mp', 'seq'), may hold values from 0.0055242716 to 0.022097087
- up_code: bfloat16 [8192, 16384], P('mp', 'seq'), may hold values from -4 to 4
- up_scale: float32 [64, 128], P('mp', 'seq'), may hold values from 0.0055242716 to 0.022097087
- down_code: bfloat16 [16384, 8192], P('seq', 'mp'), may hold values from -4 to 4
- down_scale: float32 [128, 64], P('seq', 'mp'), may hold values from 0.0078125 to 0.03125
Outputs:
- mixed: bfloat16 [128, 8192], P('seq', 'mp')
The draws below stay inside these ranges and needn't reach their ends.
All inputs are finite; a program needn't handle non-finite values.
Results may differ from the reference program's by a relative error of at most 0.0071.
Values may be sent and summed in bfloat16 or wider, within the bound.
A program may use at most 128 MiB of HBM per device.

```python
import math
import jax
import jax.numpy as jnp

D = 8192
FF = 16384
BLOCK = 128
TOKENS = 128


def level_of(key, shape, cuts, smallest, largest):
    gain = 1.0
    for dim, blocks in cuts:
        steps = jax.random.uniform(jax.random.fold_in(jax.random.fold_in(key, 6), dim), (blocks,), jnp.float32, smallest / len(cuts), largest / len(cuts))
        gain = gain * jnp.repeat(jnp.exp(steps), shape[dim] // blocks).reshape((-1,) + (1,) * (len(shape) - 1 - dim))
    return gain


def bell_draw(own_key, dims, spread, reach, split=(), kind=jnp.bfloat16):
    array = jax.random.normal(own_key, dims, jnp.float32) * spread
    if len(split) > 0:
        array = level_of(own_key, dims, split, -0.22, 0.18) * array
    return jnp.clip(array, min=-reach, max=reach).astype(kind)


def setup_inputs(seed: int = 0) -> dict:
    arg_keys = jax.random.split(jax.random.key(seed), 8)
    tokens = bell_draw(arg_keys[0], (TOKENS, D), 1.0, 6.0, ((0, 8), (1, 4)))
    gate_code = bell_draw(arg_keys[1], (D, FF), 1.0, 4.0, ((0, 4), (1, 8)))
    gate_scale = jnp.clip(jnp.exp(math.log(0.022097087) - 1.3862944 * jax.random.uniform(arg_keys[2], (D // BLOCK, FF // BLOCK), jnp.float32) ** level_of(arg_keys[2], (D // BLOCK, FF // BLOCK), ((0, 4), (1, 8)), -0.2, 0.2)), 0.0055242716, 0.022097087)
    up_code = bell_draw(arg_keys[3], (D, FF), 1.0, 4.0, ((0, 4), (1, 8)))
    up_scale = jnp.clip(jnp.exp(math.log(0.022097087) - 1.3862944 * jax.random.uniform(arg_keys[4], (D // BLOCK, FF // BLOCK), jnp.float32) ** level_of(arg_keys[4], (D // BLOCK, FF // BLOCK), ((0, 4), (1, 8)), -0.2, 0.2)), 0.0055242716, 0.022097087)
    down_code = bell_draw(arg_keys[5], (FF, D), 1.0, 4.0, ((0, 8), (1, 4)))
    down_scale = jnp.clip(jnp.exp(math.log(0.03125) - 1.3862944 * jax.random.uniform(arg_keys[6], (FF // BLOCK, D // BLOCK), jnp.float32) ** level_of(arg_keys[6], (FF // BLOCK, D // BLOCK), ((0, 8), (1, 4)), -0.2, 0.2)), 0.0078125, 0.03125)
    return dict(tokens=tokens, gate_code=gate_code, gate_scale=gate_scale, up_code=up_code, up_scale=up_scale, down_code=down_code, down_scale=down_scale)


def expand(code, scale):
    rows_all, cols_all = code.shape
    brows, bcols = scale.shape
    blocks = code.astype(jnp.float32).reshape(brows, rows_all // brows, bcols, cols_all // bcols)
    scaled = blocks * scale[:, None, :, None]
    return scaled.reshape(rows_all, cols_all).astype(jnp.bfloat16)


def reference(tokens, gate_code, gate_scale, up_code, up_scale, down_code, down_scale):
    w_gate = expand(gate_code, gate_scale)
    w_up = expand(up_code, up_scale)
    w_down = expand(down_code, down_scale)
    gate = jnp.dot(tokens, w_gate, preferred_element_type=jnp.float32)
    up = jnp.dot(tokens, w_up, preferred_element_type=jnp.float32)
    hidden = (jax.nn.silu(gate) * up).astype(jnp.bfloat16)
    return jnp.dot(hidden, w_down, preferred_element_type=jnp.float32).astype(jnp.bfloat16)
```

```python
import functools

import jax
import jax.numpy as jnp
from jax import lax
from jax.experimental import pallas as pl
from jax.experimental.pallas import tpu as pltpu
from jax.sharding import PartitionSpec as P

MESH = pl.DeviceIdType.MESH
BF16 = jnp.bfloat16
F32 = jnp.float32


def chunk_of(units):
    return 512 if units % 512 == 0 else units


def kernel(n, m, tok_hbm, wg_hbm, wu_hbm, wd_hbm, gs, us, ds, out,
           tok, wg, wu, wd, part, rsr, hid, acc, dsend, sibr, zs, zr,
           w_sem, t_loc, t_send, t_recv, f_send, f_recv,
           r_send, r_recv, h_send, h_recv, b_send, b_recv, z_send, z_recv):
    seq, mp = lax.axis_index("seq"), lax.axis_index("mp")
    nz = n // 2
    z, core = seq // 2, lax.rem(seq, 2)
    sib = z * 2 + (1 - core)
    rows_in, feats = tok_hbm.shape
    units = wg.shape[1]
    w = chunk_of(units)
    chunks = units // w
    tokens = n * rows_in
    outs = wd.shape[1]
    v = chunk_of(outs)
    vparts = outs // v
    block = feats // gs.shape[0]

    loads = {}
    for c in range(chunks):
        cols = pl.ds(c * w, w)
        for k, (src, dst) in enumerate(((wg_hbm, wg), (wu_hbm, wu))):
            loads[k, c] = pltpu.make_async_copy(src.at[:, cols], dst.at[:, cols], w_sem.at[k, c])
            loads[k, c].start()
    for c in range(chunks):
        rows = pl.ds(c * w, w)
        loads[2, c] = pltpu.make_async_copy(wd_hbm.at[rows], wd.at[rows], w_sem.at[2, c])
        loads[2, c].start()

    barrier = pltpu.get_barrier_semaphore()

    def z_peer(d):
        return lax.rem(z + d, nz) * 2 + core

    def mp_peer(d):
        return lax.rem(mp + d, m)

    for d in range(1, nz):
        pl.semaphore_signal(barrier, inc=1, device_id=(z_peer(d), mp), device_id_type=MESH)
    pl.semaphore_signal(barrier, inc=1, device_id=(sib, mp), device_id_type=MESH)
    for d in range(1, m):
        pl.semaphore_signal(barrier, inc=1, device_id=(seq, mp_peer(d)), device_id_type=MESH)
    pl.semaphore_wait(barrier, nz + m - 1)

    def remote(src, dst, ssem, rsem, to):
        return pltpu.make_async_remote_copy(
            src_ref=src, dst_ref=dst, send_sem=ssem, recv_sem=rsem,
            device_id=to, device_id_type=MESH)

    sends = []

    def tok_rows(s):
        return tok.at[pl.ds(pl.multiple_of(s * rows_in, rows_in), rows_in)]

    own = pltpu.make_async_copy(tok_hbm, tok_rows(seq), t_loc)
    own.start()
    t_copies = []
    for d in range(1, nz):
        cp = remote(tok_hbm, tok_rows(seq), t_send.at[d - 1], t_recv.at[d - 1], (z_peer(d), mp))
        cp.start()
        t_copies.append(cp)
        sends.append(cp)
    f_copies = []
    cp = remote(tok_hbm, tok_rows(seq), f_send.at[0], f_recv.at[0], (sib, mp))
    cp.start()
    f_copies.append(cp)
    sends.append(cp)

    def dequant(ref, scale, row0, nrows, col0, ncols):
        def body(i, carry):
            kb = row0 // block + i
            rows = pl.ds(pl.multiple_of(kb * block, block), block)
            for nb in range(col0 // block, (col0 + ncols) // block):
                cols = pl.ds(nb * block, block)
                ref[rows, cols] = (ref[rows, cols].astype(F32) * scale[kb, nb]).astype(BF16)
            return carry
        lax.fori_loop(0, nrows // block, body, 0)

    def prepare(c):
        loads[0, c].wait()
        dequant(wg, gs, 0, feats, c * w, w)
        loads[1, c].wait()
        dequant(wu, us, 0, feats, c * w, w)

    prepare(0)

    own.wait()
    for d in range(1, nz):
        t_copies[d - 1].wait_recv()
        s = lax.rem(z - d + nz, nz) * 2 + core
        cp = remote(tok_rows(s), tok_rows(s), f_send.at[d], f_recv.at[d], (sib, mp))
        cp.start()
        f_copies.append(cp)
        sends.append(cp)
    for cp in f_copies:
        cp.wait_recv()

    rows_mp = tokens // m

    def first(c):
        x = tok[...]
        g = jnp.dot(x, wg[:, c * w:(c + 1) * w], preferred_element_type=F32)
        part[c, :, :, :w] = g.astype(BF16).reshape(m, rows_mp, w)
        u = jnp.dot(x, wu[:, c * w:(c + 1) * w], preferred_element_type=F32)
        part[c, :, :, w:] = u.astype(BF16).reshape(m, rows_mp, w)
        copies = []
        for d in range(1, m):
            to = mp_peer(d)
            cp = remote(part.at[c, to], rsr.at[c, d - 1], r_send.at[c, d - 1],
                        r_recv.at[c, d - 1], (seq, to))
            cp.start()
            copies.append(cp)
            sends.append(cp)
        return copies

    def middle(c, copies):
        total = part[c, mp].astype(F32)
        for d in range(1, m):
            copies[d - 1].wait_recv()
            total += rsr[c, d - 1].astype(F32)
        g, u = total[:, :w], total[:, w:]
        hid[c, mp] = (g / (1.0 + jnp.exp(-g)) * u).astype(BF16)
        out_copies = []
        for d in range(1, m):
            to = mp_peer(d)
            cp = remote(hid.at[c, mp], hid.at[c, mp], h_send.at[c, d - 1],
                        h_recv.at[c, d - 1], (seq, to))
            cp.start()
            out_copies.append(cp)
            sends.append(cp)
        return out_copies

    def down(c, j):
        h = hid[c].reshape(tokens, w)
        y = jnp.dot(h, wd[c * w:(c + 1) * w, j * v:(j + 1) * v], preferred_element_type=F32)
        y = y.reshape(nz, 2, rows_in, v)
        acc[j] = y if c == 0 else acc[j] + y

    def down_all(c, copies):
        for cp in copies:
            cp.wait_recv()
        for j in range(vparts):
            down(c, j)

    rs, ag = {}, {}
    for c in range(chunks):
        if c > 0:
            prepare(c)
        rs[c] = first(c)
        loads[2, c].wait()
        dequant(wd, ds, c * w, w, 0, outs)
        if c >= 1:
            ag[c - 1] = middle(c - 1, rs[c - 1])
        if c >= 2:
            down_all(c - 2, ag[c - 2])
    last = chunks - 1
    ag[last] = middle(last, rs[last])
    if last >= 1:
        down_all(last - 1, ag[last - 1])

    for cp in ag[last]:
        cp.wait_recv()
    b_copies, z_copies = [], {}

    def across(j):
        b_copies[j].wait_recv()
        zs[j] = (acc[j, :, core] + sibr[j].astype(F32)).astype(BF16)
        for d in range(1, nz):
            cp = remote(zs.at[j, lax.rem(z + d, nz)], zr.at[j, d - 1], z_send.at[j, d - 1],
                        z_recv.at[j, d - 1], (z_peer(d), mp))
            cp.start()
            z_copies[j, d] = cp
            sends.append(cp)

    for j in range(vparts):
        down(last, j)
        dsend[j] = acc[j, :, 1 - core].astype(BF16)
        cp = remote(dsend.at[j], sibr.at[j], b_send.at[j], b_recv.at[j], (sib, mp))
        cp.start()
        b_copies.append(cp)
        sends.append(cp)
        if j >= 1:
            across(j - 1)
    across(vparts - 1)

    for j in range(vparts):
        total = acc[j, z, core] + sibr[j, z].astype(F32)
        for d in range(1, nz):
            z_copies[j, d].wait_recv()
            total += zr[j, d - 1].astype(F32)
        out[:, j * v:(j + 1) * v] = total.astype(BF16)

    for cp in sends:
        cp.wait_send()


def shards(n, m, tokens, gate_code, gate_scale, up_code, up_scale, down_code, down_scale):
    rows_in, feats = tokens.shape
    units, outs = gate_code.shape[1], down_code.shape[1]
    total = n * rows_in
    w, v = chunk_of(units), chunk_of(outs)
    chunks, vparts = units // w, outs // v
    nz, rows_mp = n // 2, total // m
    dma = pltpu.SemaphoreType.DMA
    hbm = pl.BlockSpec(memory_space=pl.ANY)
    smem = pl.BlockSpec(memory_space=pltpu.SMEM)
    return pl.pallas_call(
        functools.partial(kernel, n, m),
        out_shape=jax.ShapeDtypeStruct((rows_in, outs), BF16),
        in_specs=[hbm] * 4 + [smem] * 3,
        out_specs=pl.BlockSpec(memory_space=pltpu.VMEM),
        scratch_shapes=[
            pltpu.VMEM((total, feats), BF16),
            pltpu.VMEM((feats, units), BF16),
            pltpu.VMEM((feats, units), BF16),
            pltpu.VMEM((units, outs), BF16),
            pltpu.VMEM((chunks, m, rows_mp, 2 * w), BF16),
            pltpu.VMEM((chunks, m - 1, rows_mp, 2 * w), BF16),
            pltpu.VMEM((chunks, m, rows_mp, w), BF16),
            pltpu.VMEM((vparts, nz, 2, rows_in, v), F32),
            pltpu.VMEM((vparts, nz, rows_in, v), BF16),
            pltpu.VMEM((vparts, nz, rows_in, v), BF16),
            pltpu.VMEM((vparts, nz, rows_in, v), BF16),
            pltpu.VMEM((vparts, nz - 1, rows_in, v), BF16),
            dma((3, chunks)),
            dma,
            dma((nz - 1,)), dma((nz - 1,)),
            dma((nz,)), dma((nz,)),
            dma((chunks, m - 1)), dma((chunks, m - 1)),
            dma((chunks, m - 1)), dma((chunks, m - 1)),
            dma((vparts,)), dma((vparts,)),
            dma((vparts, nz - 1)), dma((vparts, nz - 1)),
        ],
        compiler_params=pltpu.CompilerParams(
            collective_id=0, has_side_effects=True, vmem_limit_bytes=58 * 1024 * 1024),
    )(tokens, gate_code, up_code, down_code, gate_scale, up_scale, down_scale)


def solution(mesh):
    placed = (
        P("seq", "mp"),
        P("mp", "seq"),
        P("mp", "seq"),
        P("mp", "seq"),
        P("mp", "seq"),
        P("seq", "mp"),
        P("seq", "mp"),
    )
    body = functools.partial(shards, mesh.shape["seq"], mesh.shape["mp"])
    return jax.shard_map(
        body, mesh=mesh, in_specs=placed, out_specs=P("seq", "mp"), check_vma=False
    )
```

```python
import functools

import jax
import jax.numpy as jnp
from jax import lax
from jax.experimental import pallas as pl
from jax.experimental.pallas import tpu as pltpu
from jax.sharding import PartitionSpec as P

MESH = pl.DeviceIdType.MESH
BF16 = jnp.bfloat16
F32 = jnp.float32


def chunk_of(units):
    return 512 if units % 512 == 0 else units


def units_of(units):
    return 1024 if units % 1024 == 0 else units


def kernel(n, m, tok_hbm, wg_hbm, wu_hbm, wd_hbm, gs, us, ds, out,
           tok, wg, wu, wd, part, rsr, hid, acc, dsend, sibr, zs, zr,
           w_sem, t_loc, t_send, t_recv, f_send, f_recv,
           r_send, r_recv, h_send, h_recv, b_send, b_recv, z_send, z_recv):
    seq, mp = lax.axis_index("seq"), lax.axis_index("mp")
    nz = n // 2
    z, core = seq // 2, lax.rem(seq, 2)
    sib = z * 2 + (1 - core)
    rows_in, feats = tok_hbm.shape
    units = wg.shape[1]
    w = units_of(units)
    chunks = units // w
    tokens = n * rows_in
    outs = wd.shape[1]
    v = chunk_of(outs)
    vparts = outs // v
    block = feats // gs.shape[0]

    loads = {}

    def load(k, c):
        span = pl.ds(c * w, w)
        src, dst = ((wg_hbm, wg), (wu_hbm, wu), (wd_hbm, wd))[k]
        src, dst = (src.at[span], dst.at[span]) if k == 2 else (src.at[:, span], dst.at[:, span])
        loads[k, c] = pltpu.make_async_copy(src, dst, w_sem.at[k, c])
        loads[k, c].start()

    load(0, 0)
    load(1, 0)

    barrier = pltpu.get_barrier_semaphore()

    def z_peer(d):
        return lax.rem(z + d, nz) * 2 + core

    def mp_peer(d):
        return lax.rem(mp + d, m)

    for d in range(1, nz):
        pl.semaphore_signal(barrier, inc=1, device_id=(z_peer(d), mp), device_id_type=MESH)
    pl.semaphore_signal(barrier, inc=1, device_id=(sib, mp), device_id_type=MESH)
    for d in range(1, m):
        pl.semaphore_signal(barrier, inc=1, device_id=(seq, mp_peer(d)), device_id_type=MESH)
    pl.semaphore_wait(barrier, nz + m - 1)

    def remote(src, dst, ssem, rsem, to):
        return pltpu.make_async_remote_copy(
            src_ref=src, dst_ref=dst, send_sem=ssem, recv_sem=rsem,
            device_id=to, device_id_type=MESH)

    sends = []

    def tok_rows(s):
        return tok.at[lax.rem(s, 2), pl.ds(pl.multiple_of(s // 2 * rows_in, rows_in), rows_in)]

    own = pltpu.make_async_copy(tok_hbm, tok_rows(seq), t_loc)
    own.start()
    t_copies = []
    for d in range(1, nz):
        cp = remote(tok_hbm, tok_rows(seq), t_send.at[d - 1], t_recv.at[d - 1], (z_peer(d), mp))
        cp.start()
        t_copies.append(cp)
        sends.append(cp)
    f_copies = []
    cp = remote(tok_hbm, tok_rows(seq), f_send.at[0], f_recv.at[0], (sib, mp))
    cp.start()
    f_copies.append(cp)
    sends.append(cp)

    for c in range(1, chunks):
        load(0, c)
        load(1, c)
    for c in range(chunks):
        load(2, c)

    def dequant(ref, scale, row0, nrows, col0, ncols):
        def body(i, carry):
            kb = row0 // block + i
            rows = pl.ds(pl.multiple_of(kb * block, block), block)
            for nb in range(col0 // block, (col0 + ncols) // block):
                cols = pl.ds(nb * block, block)
                ref[rows, cols] = (ref[rows, cols].astype(F32) * scale[kb, nb]).astype(BF16)
            return carry
        lax.fori_loop(0, nrows // block, body, 0)

    def prepare(c):
        loads[0, c].wait()
        dequant(wg, gs, 0, feats, c * w, w)
        loads[1, c].wait()
        dequant(wu, us, 0, feats, c * w, w)

    prepare(0)

    own.wait()
    for d in range(1, nz):
        t_copies[d - 1].wait_recv()
        s = lax.rem(z - d + nz, nz) * 2 + core
        cp = remote(tok_rows(s), tok_rows(s), f_send.at[d], f_recv.at[d], (sib, mp))
        cp.start()
        f_copies.append(cp)
        sends.append(cp)
    for cp in f_copies:
        cp.wait_recv()

    half = tokens // 2
    rows_mp = half // m

    def first(h, c):
        x = tok[h]
        g = jnp.dot(x, wg[:, c * w:(c + 1) * w], preferred_element_type=F32)
        part[h, c, :, :, :w] = g.astype(BF16).reshape(m, rows_mp, w)
        u = jnp.dot(x, wu[:, c * w:(c + 1) * w], preferred_element_type=F32)
        part[h, c, :, :, w:] = u.astype(BF16).reshape(m, rows_mp, w)
        copies = []
        for d in range(1, m):
            to = mp_peer(d)
            cp = remote(part.at[h, c, to], rsr.at[h, c, d - 1], r_send.at[h, c, d - 1],
                        r_recv.at[h, c, d - 1], (seq, to))
            cp.start()
            copies.append(cp)
            sends.append(cp)
        rs[h, c] = copies

    def middle(h, c):
        total = part[h, c, mp].astype(F32)
        for d in range(1, m):
            rs[h, c][d - 1].wait_recv()
            total += rsr[h, c, d - 1].astype(F32)
        g, u = total[:, :w], total[:, w:]
        hid[h, c, mp] = (g / (1.0 + jnp.exp(-g)) * u).astype(BF16)
        copies = []
        for d in range(1, m):
            to = mp_peer(d)
            cp = remote(hid.at[h, c, mp], hid.at[h, c, mp], h_send.at[h, c, d - 1],
                        h_recv.at[h, c, d - 1], (seq, to))
            cp.start()
            copies.append(cp)
            sends.append(cp)
        ag[h, c] = copies

    def down(h, c, j):
        x = hid[h, c].reshape(half, w)
        y = jnp.dot(x, wd[c * w:(c + 1) * w, j * v:(j + 1) * v], preferred_element_type=F32)
        y = y.reshape(nz, rows_in, v)
        acc[h, j] = y if c == 0 else acc[h, j] + y

    def to_sibling(j):
        return remote(dsend.at[j], sibr.at[j], b_send.at[j], b_recv.at[j], (sib, mp))

    def to_z(j, d):
        return remote(zs.at[j, lax.rem(z + d, nz)], zr.at[j, d - 1], z_send.at[j, d - 1],
                      z_recv.at[j, d - 1], (z_peer(d), mp))

    def down_half(h):
        for c in range(chunks - 1):
            for cp in ag[h, c]:
                cp.wait_recv()
            for j in range(vparts):
                down(h, c, j)
        for cp in ag[h, chunks - 1]:
            cp.wait_recv()
        for j in range(vparts):
            down(h, chunks - 1, j)

            @pl.when(core == 1 - h)
            def _():
                dsend[j] = acc[h, j].astype(BF16)
                to_sibling(j).start()

    def across(h):
        @pl.when(core == h)
        def _():
            for j in range(vparts):
                to_sibling(j).wait_recv()
                zs[j] = (acc[h, j] + sibr[j].astype(F32)).astype(BF16)
                for d in range(1, nz):
                    to_z(j, d).start()

    rs, ag = {}, {}
    for c in range(chunks):
        if c > 0:
            prepare(c)
        first(0, c)
    for c in range(chunks):
        first(1, c)
        middle(0, c)
    for c in range(chunks):
        loads[2, c].wait()
        dequant(wd, ds, c * w, w, 0, outs)
    for c in range(chunks):
        middle(1, c)
    down_half(0)
    across(0)
    down_half(1)
    across(1)

    for j in range(vparts):
        total = acc[core, j, z] + sibr[j, z].astype(F32)
        for d in range(1, nz):
            to_z(j, d).wait_recv()
            total += zr[j, d - 1].astype(F32)
        out[:, j * v:(j + 1) * v] = total.astype(BF16)

    for j in range(vparts):
        to_sibling(j).wait_send()
        for d in range(1, nz):
            to_z(j, d).wait_send()
    for cp in sends:
        cp.wait_send()


def shards(n, m, tokens, gate_code, gate_scale, up_code, up_scale, down_code, down_scale):
    rows_in, feats = tokens.shape
    units, outs = gate_code.shape[1], down_code.shape[1]
    total = n * rows_in
    w, v = units_of(units), chunk_of(outs)
    chunks, vparts = units // w, outs // v
    nz, rows_mp = n // 2, total // 2 // m
    dma = pltpu.SemaphoreType.DMA
    hbm = pl.BlockSpec(memory_space=pl.ANY)
    smem = pl.BlockSpec(memory_space=pltpu.SMEM)
    return pl.pallas_call(
        functools.partial(kernel, n, m),
        out_shape=jax.ShapeDtypeStruct((rows_in, outs), BF16),
        in_specs=[hbm] * 4 + [smem] * 3,
        out_specs=pl.BlockSpec(memory_space=pltpu.VMEM),
        scratch_shapes=[
            pltpu.VMEM((2, total // 2, feats), BF16),
            pltpu.VMEM((feats, units), BF16),
            pltpu.VMEM((feats, units), BF16),
            pltpu.VMEM((units, outs), BF16),
            pltpu.VMEM((2, chunks, m, rows_mp, 2 * w), BF16),
            pltpu.VMEM((2, chunks, m - 1, rows_mp, 2 * w), BF16),
            pltpu.VMEM((2, chunks, m, rows_mp, w), BF16),
            pltpu.VMEM((2, vparts, nz, rows_in, v), F32),
            pltpu.VMEM((vparts, nz, rows_in, v), BF16),
            pltpu.VMEM((vparts, nz, rows_in, v), BF16),
            pltpu.VMEM((vparts, nz, rows_in, v), BF16),
            pltpu.VMEM((vparts, nz - 1, rows_in, v), BF16),
            dma((3, chunks)),
            dma,
            dma((nz - 1,)), dma((nz - 1,)),
            dma((nz,)), dma((nz,)),
            dma((2, chunks, m - 1)), dma((2, chunks, m - 1)),
            dma((2, chunks, m - 1)), dma((2, chunks, m - 1)),
            dma((vparts,)), dma((vparts,)),
            dma((vparts, nz - 1)), dma((vparts, nz - 1)),
        ],
        compiler_params=pltpu.CompilerParams(
            collective_id=0, has_side_effects=True, vmem_limit_bytes=58 * 1024 * 1024),
    )(tokens, gate_code, up_code, down_code, gate_scale, up_scale, down_scale)


def solution(mesh):
    placed = (
        P("seq", "mp"),
        P("mp", "seq"),
        P("mp", "seq"),
        P("mp", "seq"),
        P("mp", "seq"),
        P("seq", "mp"),
        P("seq", "mp"),
    )
    body = functools.partial(shards, mesh.shape["seq"], mesh.shape["mp"])
    return jax.shard_map(
        body, mesh=mesh, in_specs=placed, out_specs=P("seq", "mp"), check_vma=False
    )
```

```python
import functools

import jax
import jax.numpy as jnp
from jax import lax
from jax.experimental import pallas as pl
from jax.experimental.pallas import tpu as pltpu
from jax.sharding import PartitionSpec as P

MESH = pl.DeviceIdType.MESH
BF16 = jnp.bfloat16
F32 = jnp.float32


def chunk_of(units):
    return 512 if units % 512 == 0 else units


def units_of(units):
    return 1024 if units % 1024 == 0 else units


def kernel(n, m, tok_hbm, wg_hbm, wu_hbm, wd_hbm, gs, us, ds, out,
           tok, wg, wu, wd, part, rsr, hid, acc, dsend, sibr, zs, zr,
           w_sem, t_loc, t_send, t_recv, f_send, f_recv,
           r_send, r_recv, h_send, h_recv, b_send, b_recv, z_send, z_recv):
    seq, mp = lax.axis_index("seq"), lax.axis_index("mp")
    nz = n // 2
    z, core = seq // 2, lax.rem(seq, 2)
    sib = z * 2 + (1 - core)
    rows_in, feats = tok_hbm.shape
    units = wg.shape[1]
    w = units_of(units)
    chunks = units // w
    tokens = n * rows_in
    outs = wd.shape[1]
    v = chunk_of(outs)
    vparts = outs // v
    block = feats // gs.shape[0]

    loads = {}

    def load(k, c):
        span = pl.ds(c * w, w)
        src, dst = ((wg_hbm, wg), (wu_hbm, wu), (wd_hbm, wd))[k]
        src, dst = (src.at[span], dst.at[span]) if k == 2 else (src.at[:, span], dst.at[:, span])
        loads[k, c] = pltpu.make_async_copy(src, dst, w_sem.at[k, c])
        loads[k, c].start()

    load(0, 0)
    load(1, 0)

    barrier = pltpu.get_barrier_semaphore()

    def z_peer(d):
        return lax.rem(z + d, nz) * 2 + core

    def mp_peer(d):
        return lax.rem(mp + d, m)

    for d in range(1, nz):
        pl.semaphore_signal(barrier, inc=1, device_id=(z_peer(d), mp), device_id_type=MESH)
    pl.semaphore_signal(barrier, inc=1, device_id=(sib, mp), device_id_type=MESH)
    for d in range(1, m):
        pl.semaphore_signal(barrier, inc=1, device_id=(seq, mp_peer(d)), device_id_type=MESH)
    pl.semaphore_wait(barrier, nz + m - 1)

    def remote(src, dst, ssem, rsem, to):
        return pltpu.make_async_remote_copy(
            src_ref=src, dst_ref=dst, send_sem=ssem, recv_sem=rsem,
            device_id=to, device_id_type=MESH)

    sends = []

    def tok_rows(s):
        return tok.at[lax.rem(s, 2), pl.ds(pl.multiple_of(s // 2 * rows_in, rows_in), rows_in)]

    own = pltpu.make_async_copy(tok_hbm, tok_rows(seq), t_loc)
    own.start()
    t_copies = []
    for d in range(1, nz):
        cp = remote(tok_hbm, tok_rows(seq), t_send.at[d - 1], t_recv.at[d - 1], (z_peer(d), mp))
        cp.start()
        t_copies.append(cp)
        sends.append(cp)
    f_copies = []
    cp = remote(tok_hbm, tok_rows(seq), f_send.at[0], f_recv.at[0], (sib, mp))
    cp.start()
    f_copies.append(cp)
    sends.append(cp)

    for c in range(1, chunks):
        load(0, c)
        load(1, c)
    for c in range(chunks):
        load(2, c)

    def dequant(ref, scale, row0, nrows, col0, ncols):
        def body(i, carry):
            kb = row0 // block + i
            rows = pl.ds(pl.multiple_of(kb * block, block), block)
            for nb in range(col0 // block, (col0 + ncols) // block):
                cols = pl.ds(nb * block, block)
                ref[rows, cols] = (ref[rows, cols].astype(F32) * scale[kb, nb]).astype(BF16)
            return carry
        lax.fori_loop(0, nrows // block, body, 0)

    def prepare(c):
        loads[0, c].wait()
        dequant(wg, gs, 0, feats, c * w, w)
        loads[1, c].wait()
        dequant(wu, us, 0, feats, c * w, w)

    prepare(0)

    own.wait()
    for d in range(1, nz):
        t_copies[d - 1].wait_recv()
        s = lax.rem(z - d + nz, nz) * 2 + core
        cp = remote(tok_rows(s), tok_rows(s), f_send.at[d], f_recv.at[d], (sib, mp))
        cp.start()
        f_copies.append(cp)
        sends.append(cp)
    for cp in f_copies:
        cp.wait_recv()

    half = tokens // 2
    rows_mp = half // m

    def first(h, c):
        x = tok[h]
        g = jnp.dot(x, wg[:, c * w:(c + 1) * w], preferred_element_type=F32)
        part[h, c, :, :, :w] = g.astype(BF16).reshape(m, rows_mp, w)
        u = jnp.dot(x, wu[:, c * w:(c + 1) * w], preferred_element_type=F32)
        part[h, c, :, :, w:] = u.astype(BF16).reshape(m, rows_mp, w)
        copies = []
        for d in range(1, m):
            to = mp_peer(d)
            cp = remote(part.at[h, c, to], rsr.at[h, c, d - 1], r_send.at[h, c, d - 1],
                        r_recv.at[h, c, d - 1], (seq, to))
            cp.start()
            copies.append(cp)
            sends.append(cp)
        rs[h, c] = copies

    def middle(h, c):
        total = part[h, c, mp].astype(F32)
        for d in range(1, m):
            rs[h, c][d - 1].wait_recv()
            total += rsr[h, c, d - 1].astype(F32)
        g, u = total[:, :w], total[:, w:]
        hid[h, c, mp] = (g / (1.0 + jnp.exp(-g)) * u).astype(BF16)
        copies = []
        for d in range(1, m):
            to = mp_peer(d)
            cp = remote(hid.at[h, c, mp], hid.at[h, c, mp], h_send.at[h, c, d - 1],
                        h_recv.at[h, c, d - 1], (seq, to))
            cp.start()
            copies.append(cp)
            sends.append(cp)
        ag[h, c] = copies

    def down(h, c, j):
        x = hid[h, c].reshape(half, w)
        y = jnp.dot(x, wd[c * w:(c + 1) * w, j * v:(j + 1) * v], preferred_element_type=F32)
        y = y.reshape(nz, rows_in, v)
        acc[h, j] = y if c == 0 else acc[h, j] + y

    def to_sibling(j):
        return remote(dsend.at[j], sibr.at[j], b_send.at[j], b_recv.at[j], (sib, mp))

    def to_z(j, d):
        return remote(zs.at[j, lax.rem(z + d, nz)], zr.at[j, d - 1], z_send.at[j, d - 1],
                      z_recv.at[j, d - 1], (z_peer(d), mp))

    def down_half(h):
        for c in range(chunks - 1):
            for cp in ag[h, c]:
                cp.wait_recv()
            for j in range(vparts):
                down(h, c, j)
        for cp in ag[h, chunks - 1]:
            cp.wait_recv()
        for j in range(vparts):
            down(h, chunks - 1, j)

            @pl.when(core == 1 - h)
            def _():
                dsend[j] = acc[h, j].astype(BF16)
                to_sibling(j).start()

    def across(h):
        @pl.when(core == h)
        def _():
            for j in range(vparts):
                to_sibling(j).wait_recv()
                zs[j] = (acc[h, j] + sibr[j].astype(F32)).astype(BF16)
                for d in range(1, nz):
                    to_z(j, d).start()

    rs, ag = {}, {}
    for c in range(chunks):
        if c > 0:
            prepare(c)
        first(0, c)
        first(1, c)
    for c in range(chunks):
        loads[2, c].wait()
        dequant(wd, ds, c * w, w, 0, outs)
        middle(0, c)
    for c in range(chunks):
        middle(1, c)
    down_half(0)
    across(0)
    down_half(1)
    across(1)

    for j in range(vparts):
        total = acc[core, j, z] + sibr[j, z].astype(F32)
        for d in range(1, nz):
            to_z(j, d).wait_recv()
            total += zr[j, d - 1].astype(F32)
        out[:, j * v:(j + 1) * v] = total.astype(BF16)

    for j in range(vparts):
        to_sibling(j).wait_send()
        for d in range(1, nz):
            to_z(j, d).wait_send()
    for cp in sends:
        cp.wait_send()


def shards(n, m, tokens, gate_code, gate_scale, up_code, up_scale, down_code, down_scale):
    rows_in, feats = tokens.shape
    units, outs = gate_code.shape[1], down_code.shape[1]
    total = n * rows_in
    w, v = units_of(units), chunk_of(outs)
    chunks, vparts = units // w, outs // v
    nz, rows_mp = n // 2, total // 2 // m
    dma = pltpu.SemaphoreType.DMA
    hbm = pl.BlockSpec(memory_space=pl.ANY)
    smem = pl.BlockSpec(memory_space=pltpu.SMEM)
    return pl.pallas_call(
        functools.partial(kernel, n, m),
        out_shape=jax.ShapeDtypeStruct((rows_in, outs), BF16),
        in_specs=[hbm] * 4 + [smem] * 3,
        out_specs=pl.BlockSpec(memory_space=pltpu.VMEM),
        scratch_shapes=[
            pltpu.VMEM((2, total // 2, feats), BF16),
            pltpu.VMEM((feats, units), BF16),
            pltpu.VMEM((feats, units), BF16),
            pltpu.VMEM((units, outs), BF16),
            pltpu.VMEM((2, chunks, m, rows_mp, 2 * w), BF16),
            pltpu.VMEM((2, chunks, m - 1, rows_mp, 2 * w), BF16),
            pltpu.VMEM((2, chunks, m, rows_mp, w), BF16),
            pltpu.VMEM((2, vparts, nz, rows_in, v), F32),
            pltpu.VMEM((vparts, nz, rows_in, v), BF16),
            pltpu.VMEM((vparts, nz, rows_in, v), BF16),
            pltpu.VMEM((vparts, nz, rows_in, v), BF16),
            pltpu.VMEM((vparts, nz - 1, rows_in, v), BF16),
            dma((3, chunks)),
            dma,
            dma((nz - 1,)), dma((nz - 1,)),
            dma((nz,)), dma((nz,)),
            dma((2, chunks, m - 1)), dma((2, chunks, m - 1)),
            dma((2, chunks, m - 1)), dma((2, chunks, m - 1)),
            dma((vparts,)), dma((vparts,)),
            dma((vparts, nz - 1)), dma((vparts, nz - 1)),
        ],
        compiler_params=pltpu.CompilerParams(
            collective_id=0, has_side_effects=True, vmem_limit_bytes=58 * 1024 * 1024),
    )(tokens, gate_code, up_code, down_code, gate_scale, up_scale, down_scale)


def solution(mesh):
    placed = (
        P("seq", "mp"),
        P("mp", "seq"),
        P("mp", "seq"),
        P("mp", "seq"),
        P("mp", "seq"),
        P("seq", "mp"),
        P("seq", "mp"),
    )
    body = functools.partial(shards, mesh.shape["seq"], mesh.shape["mp"])
    return jax.shard_map(
        body, mesh=mesh, in_specs=placed, out_specs=P("seq", "mp"), check_vma=False
    )
```
